32 devices in a mesh: aux: 8 (over z, y), occ: 4 (over x, core).
Axes of the slice: x: 2, y: 2, z: 4, core: 2. Of those that a mesh axis runs over, the one named last changes fastest.
Arguments:
- factors: bfloat16 [256, 128, 384], P('occ', 'aux'), may hold values from -1 to 1
- response: bfloat16 [256, 128, 384], P('occ', 'aux'), may hold values from -1 to 1
- pattern: int32 [3, 3], replicated, may hold values 0 or 1
Outputs:
- exchange_k: float32 [384, 384], P('aux', 'occ')
The draws below stay inside these ranges and needn't reach their ends.
All inputs are finite; a program needn't handle non-finite values.
Results may differ from the reference program's by a relative error of at most 0.0003.
Values sent between devices are 32-bit elements; how exact they have to be, the bound alone decides.
No kernel may reach another device: no remote copies, remote signals or barrier semaphores. Data moves between devices by JAX's collectives and lax.ppermute only.
A program may use at most 64 MiB of HBM per device.

```python
import jax
import jax.numpy as jnp
from jax import lax

NOCC = 256
BLK = 128
NBAS = 384
NAUX = 128
NB = 3


def touch_ends(drawn, rng, least, largest):
    place = [jax.random.randint(jax.random.fold_in(rng, axis), (), 0, length) for axis, length in enumerate(drawn.shape)]
    longest = drawn.shape.index(max(drawn.shape))
    neighbour = place[:longest] + [(place[longest] + 1) % drawn.shape[longest]] + place[longest + 1:]
    return drawn.at[tuple(place)].set(least).at[tuple(neighbour)].set(largest)


def steps_of(own_key, extent, shards, least, high):
    level = 1.0
    for axis_at, parts in shards:
        draws = jax.random.uniform(jax.random.fold_in(jax.random.fold_in(own_key, 6), axis_at), (parts,), jnp.float32, least / len(shards), high / len(shards))
        level = level * jnp.repeat(jnp.exp(draws), extent[axis_at] // parts).reshape((-1,) + (1,) * (len(extent) - 1 - axis_at))
    return level


def bell_draw(stream_key, dims, deviation, most, pieces=(), held_as=jnp.bfloat16):
    factor_of = steps_of(stream_key, dims, pieces, -0.22, 0.18) if pieces else 1.0
    drawn = jax.random.normal(stream_key, dims, jnp.float32) * deviation * factor_of
    return jnp.minimum(jnp.maximum(drawn, -most), most).astype(held_as)


def setup_inputs(seed: int = 0) -> dict:
    arg_keys = jax.random.split(jax.random.key(seed), 4)
    return {
        "factors": bell_draw(arg_keys[0], (NOCC, NAUX, NBAS), ((NAUX * NOCC) ** -0.25), 1.0, ((0, 4), (1, 8))),
        "response": bell_draw(arg_keys[1], (NOCC, NAUX, NBAS), ((NAUX * NOCC) ** -0.25), 1.0, ((0, 4), (1, 8))),
        "pattern": touch_ends((jax.random.randint(arg_keys[2], (NB, NB), 0, 2) < 1).astype(jnp.int32), jax.random.fold_in(arg_keys[2], 1), 0, 1),
    }


def expand_tiles(pattern):
    tile_table = pattern.astype(jnp.float32)
    return jnp.repeat(jnp.repeat(tile_table, BLK, axis=0), BLK, axis=1)


def reference(factors, response, pattern):
    ground_rows = factors.reshape(NOCC * NAUX, NBAS)
    response_rows = response.reshape(NOCC * NAUX, NBAS)
    product = lax.dot_general(ground_rows, response_rows, (((0,), (0,)), ((), ())), preferred_element_type=jnp.float32)
    masked = expand_tiles(pattern) * product
    return 0.5 * (masked + masked.T)
```

```python
import functools

import jax
import jax.numpy as jnp
from jax import lax
from jax.experimental import pallas as pl
from jax.experimental.pallas import tpu as pltpu
from jax.sharding import PartitionSpec as P

BOTH = ("aux", "occ")
CORE, X, Y, Z1, Z2 = 1, 2, 4, 8, 16
PLANE = (X | Y | CORE, X, Y | CORE)
LINE = (Z1 | Z2 | CORE, Z2 | CORE, Z1)
CHUNKS = 4


def swap(value, mask):
    return lax.ppermute(value, BOTH, [(i, i ^ mask) for i in range(32)])


def pack_kernel(pattern_hbm, ground_hbm, response_hbm, away_ref, stay_ref, ground, response, pattern, product, tiles, sems):
    depth, nbasis = ground.shape
    step = depth // CHUNKS
    nblocks = pattern.shape[0]
    blk = nbasis // nblocks
    rows, cols = nbasis // 8, nbasis // 4
    part = cols // 3

    copies = []
    for k in range(CHUNKS):
        here = pl.ds(k * step, step)
        copies.append(pltpu.make_async_copy(ground_hbm.at[here], ground.at[here], sems.at[2 * k]))
        copies.append(pltpu.make_async_copy(response_hbm.at[here], response.at[here], sems.at[2 * k + 1]))
    masks = pltpu.make_async_copy(pattern_hbm, pattern, sems.at[2 * CHUNKS])
    for copy in copies:
        copy.start()
    masks.start()
    for k in range(CHUNKS):
        copies[2 * k].wait()
        copies[2 * k + 1].wait()
        here = pl.ds(k * step, step)
        term = lax.dot_general(
            ground[here, :], response[here, :], (((0,), (0,)), ((), ())), preferred_element_type=jnp.float32
        )
        if k == 0:
            product[...] = term
        else:
            product[...] += term
    masks.wait()

    for i in range(nblocks):
        for j in range(i, nblocks):
            upper = 0.5 * pattern[i, j].astype(jnp.float32)
            lower = 0.5 * pattern[j, i].astype(jnp.float32)
            at_i, at_j = slice(i * blk, (i + 1) * blk), slice(j * blk, (j + 1) * blk)
            both = upper * product[at_i, at_j] + lower * product[at_j, at_i].T
            product[at_i, at_j] = both
            if i != j:
                product[at_j, at_i] = both.T
    for o in range(4):
        tiles[o, :, 0:cols] = product[:, o * cols : (o + 1) * cols]

    aux, occ = lax.axis_index("aux"), lax.axis_index("occ")
    z, y, x, core = aux // 2, aux % 2, occ // 2, occ % 2
    kind = core ^ y ^ (z // 2)
    lane = lax.broadcasted_iota(jnp.int32, (rows, 128), 1)
    for out_ref, flip in ((away_ref, 1), (stay_ref, 0)):
        for group in range(4):
            x_to, y_to = x ^ (group % 2), y ^ (group // 2)
            picked = []
            for turn in range(4):
                z_to = z ^ turn
                core_to = kind ^ flip ^ y_to ^ (z_to // 2)
                picked.append(tiles[2 * x_to + core_to, pl.ds(rows * (2 * z_to + y_to), rows), :])
            for turn in (1, 2, 3):
                own = pltpu.roll(picked[0], cols - part * (turn - 1), 1)
                at = group * 3 * rows + (turn - 1) * rows
                out_ref[pl.ds(at, rows), :] = jnp.where(lane < cols, picked[turn], own)


def fast_shards(factors, response, pattern):
    nocc_dev, aux_dev, nbasis = factors.shape
    depth = nocc_dev * aux_dev
    rows, cols = nbasis // 8, nbasis // 4
    part = cols // 3
    half = jax.ShapeDtypeStruct((12 * rows, 128), jnp.float32)
    away, stay = pl.pallas_call(
        pack_kernel,
        out_shape=(half, half),
        in_specs=[pl.BlockSpec(memory_space=pl.ANY)] * 3,
        out_specs=(pl.BlockSpec(memory_space=pltpu.VMEM),) * 2,
        scratch_shapes=[
            pltpu.VMEM((depth, nbasis), jnp.bfloat16),
            pltpu.VMEM((depth, nbasis), jnp.bfloat16),
            pltpu.SMEM(pattern.shape, jnp.int32),
            pltpu.VMEM((nbasis, nbasis), jnp.float32),
            pltpu.VMEM((4, nbasis, 128), jnp.float32),
            pltpu.SemaphoreType.DMA((2 * CHUNKS + 1,)),
        ],
        compiler_params=pltpu.CompilerParams(vmem_limit_bytes=32 * 1024 * 1024),
    )(pattern, factors.reshape(depth, nbasis), response.reshape(depth, nbasis))
    chip = (stay + swap(away, CORE)).reshape(4, 3 * rows, 128)
    order = {X: 1, Y | CORE: 2, X | Y | CORE: 3}
    plane = [swap(chip[order[mask]], mask) for mask in PLANE]
    line = (chip[0] + plane[0] + plane[1] + plane[2]).reshape(3, rows, 128)
    turns = {Z1: 0, Z2 | CORE: 1, Z1 | Z2 | CORE: 2}
    last = [swap(line[turns[mask]], mask) for mask in LINE]
    own = jnp.concatenate([line[0, :, cols:], line[1, :, cols:], line[2, :, cols:]], axis=1)
    return own + last[0][:, :cols] + last[1][:, :cols] + last[2][:, :cols]


def any_shards(factors, response, pattern):
    nocc_dev, aux_dev, nbasis = factors.shape
    ground_rows = factors.reshape(nocc_dev * aux_dev, nbasis)
    response_rows = response.reshape(nocc_dev * aux_dev, nbasis)
    blk = nbasis // pattern.shape[0]
    own_cols = nbasis // lax.axis_size("occ")
    cross = lax.dot_general(
        ground_rows, response_rows, (((0,), (0,)), ((), ())), preferred_element_type=jnp.float32
    )
    masked = jnp.repeat(jnp.repeat(pattern.astype(jnp.float32), blk, axis=0), blk, axis=1) * cross
    both = 0.5 * (masked + masked.T)
    own_rows = lax.psum_scatter(both, "aux", scatter_dimension=0, tiled=True)
    summed = lax.psum(own_rows, "occ")
    return lax.dynamic_slice_in_dim(summed, lax.axis_index("occ") * own_cols, own_cols, 1)


def solution(mesh):
    in_specs = (P("occ", "aux", None), P("occ", "aux", None), P())
    out_specs = P("aux", "occ")
    sizes = dict(mesh.shape)
    shards = fast_shards if sizes["aux"] == 8 and sizes["occ"] == 4 else any_shards
    return jax.shard_map(shards, mesh=mesh, in_specs=in_specs, out_specs=out_specs, check_vma=False)
```

```python
import functools

import jax
import jax.numpy as jnp
from jax import lax
from jax.experimental import pallas as pl
from jax.experimental.pallas import tpu as pltpu
from jax.sharding import PartitionSpec as P

BOTH = ("aux", "occ")
CORE, X, Y, Z1, Z2 = 1, 2, 4, 8, 16
PLANE = (X | Y | CORE, X, Y | CORE)
LINE = (Z1 | Z2 | CORE, Z2 | CORE, Z1)
CHUNKS = 2


def swap(value, mask):
    return lax.ppermute(value, BOTH, [(i, i ^ mask) for i in range(32)])


def pack_kernel(pattern_hbm, ground_hbm, response_hbm, away_ref, stay_ref, ground, response, pattern, product, tiles, sems):
    depth, nbasis = ground.shape
    step = depth // CHUNKS
    nblocks = pattern.shape[0]
    blk = nbasis // nblocks
    rows, cols = nbasis // 8, nbasis // 4
    part = cols // 3

    copies = []
    for k in range(CHUNKS):
        here = pl.ds(k * step, step)
        copies.append(pltpu.make_async_copy(ground_hbm.at[here], ground.at[here], sems.at[2 * k]))
        copies.append(pltpu.make_async_copy(response_hbm.at[here], response.at[here], sems.at[2 * k + 1]))
    masks = pltpu.make_async_copy(pattern_hbm, pattern, sems.at[2 * CHUNKS])
    for copy in copies:
        copy.start()
    masks.start()
    for copy in copies:
        copy.wait()
    product[...] = lax.dot_general(
        ground[...], response[...], (((0,), (0,)), ((), ())), preferred_element_type=jnp.float32
    )
    masks.wait()

    for i in range(nblocks):
        for j in range(i, nblocks):
            upper = 0.5 * pattern[i, j].astype(jnp.float32)
            lower = 0.5 * pattern[j, i].astype(jnp.float32)
            at_i, at_j = slice(i * blk, (i + 1) * blk), slice(j * blk, (j + 1) * blk)
            both = upper * product[at_i, at_j] + lower * product[at_j, at_i].T
            product[at_i, at_j] = both
            if i != j:
                product[at_j, at_i] = both.T
    for o in range(4):
        tiles[o, :, 0:cols] = product[:, o * cols : (o + 1) * cols]

    aux, occ = lax.axis_index("aux"), lax.axis_index("occ")
    z, y, x, core = aux // 2, aux % 2, occ // 2, occ % 2
    kind = core ^ y ^ (z // 2)
    lane = lax.broadcasted_iota(jnp.int32, (rows, 128), 1)
    for out_ref, flip in ((away_ref, 1), (stay_ref, 0)):
        for group in range(4):
            x_to, y_to = x ^ (group % 2), y ^ (group // 2)
            picked = []
            for turn in range(4):
                z_to = z ^ turn
                core_to = kind ^ flip ^ y_to ^ (z_to // 2)
                picked.append(tiles[2 * x_to + core_to, pl.ds(rows * (2 * z_to + y_to), rows), :])
            for turn in (1, 2, 3):
                own = pltpu.roll(picked[0], cols - part * (turn - 1), 1)
                at = group * 3 * rows + (turn - 1) * rows
                out_ref[pl.ds(at, rows), :] = jnp.where(lane < cols, picked[turn], own)


def fast_shards(factors, response, pattern):
    nocc_dev, aux_dev, nbasis = factors.shape
    depth = nocc_dev * aux_dev
    rows, cols = nbasis // 8, nbasis // 4
    ground_rows = factors.reshape(depth, nbasis)
    response_rows = response.reshape(depth, nbasis)
    half = jax.ShapeDtypeStruct((12 * rows, 128), jnp.float32)
    away, stay = pl.pallas_call(
        pack_kernel,
        out_shape=(half, half),
        in_specs=[pl.BlockSpec(memory_space=pltpu.HBM)] * 3,
        out_specs=(pl.BlockSpec(memory_space=pltpu.VMEM),) * 2,
        scratch_shapes=[
            pltpu.VMEM((depth, nbasis), jnp.bfloat16),
            pltpu.VMEM((depth, nbasis), jnp.bfloat16),
            pltpu.SMEM(pattern.shape, jnp.int32),
            pltpu.VMEM((nbasis, nbasis), jnp.float32),
            pltpu.VMEM((4, nbasis, 128), jnp.float32),
            pltpu.SemaphoreType.DMA((2 * CHUNKS + 1,)),
        ],
        compiler_params=pltpu.CompilerParams(vmem_limit_bytes=32 * 1024 * 1024),
    )(*(pltpu.with_memory_space_constraint(a, pltpu.HBM) for a in (pattern, ground_rows, response_rows)))
    chip = (stay + swap(away, CORE)).reshape(4, 3 * rows, 128)
    order = {X: 1, Y | CORE: 2, X | Y | CORE: 3}
    plane = [swap(chip[order[mask]], mask) for mask in PLANE]
    line = (chip[0] + plane[0] + plane[1] + plane[2]).reshape(3, rows, 128)
    turns = {Z1: 0, Z2 | CORE: 1, Z1 | Z2 | CORE: 2}
    last = [swap(line[turns[mask]], mask) for mask in LINE]
    own = jnp.concatenate([line[0, :, cols:], line[1, :, cols:], line[2, :, cols:]], axis=1)
    return own + last[0][:, :cols] + last[1][:, :cols] + last[2][:, :cols]


def any_shards(factors, response, pattern):
    nocc_dev, aux_dev, nbasis = factors.shape
    ground_rows = factors.reshape(nocc_dev * aux_dev, nbasis)
    response_rows = response.reshape(nocc_dev * aux_dev, nbasis)
    blk = nbasis // pattern.shape[0]
    own_cols = nbasis // lax.axis_size("occ")
    cross = lax.dot_general(
        ground_rows, response_rows, (((0,), (0,)), ((), ())), preferred_element_type=jnp.float32
    )
    masked = jnp.repeat(jnp.repeat(pattern.astype(jnp.float32), blk, axis=0), blk, axis=1) * cross
    both = 0.5 * (masked + masked.T)
    own_rows = lax.psum_scatter(both, "aux", scatter_dimension=0, tiled=True)
    summed = lax.psum(own_rows, "occ")
    return lax.dynamic_slice_in_dim(summed, lax.axis_index("occ") * own_cols, own_cols, 1)


def solution(mesh):
    in_specs = (P("occ", "aux", None), P("occ", "aux", None), P())
    out_specs = P("aux", "occ")
    sizes = dict(mesh.shape)
    shards = fast_shards if sizes["aux"] == 8 and sizes["occ"] == 4 else any_shards
    return jax.shard_map(shards, mesh=mesh, in_specs=in_specs, out_specs=out_specs, check_vma=False)
```

```python
import functools

import jax
import jax.numpy as jnp
from jax import lax
from jax.experimental import pallas as pl
from jax.experimental.pallas import tpu as pltpu
from jax.sharding import PartitionSpec as P

BOTH = ("aux", "occ")
FLIPS = (((0, 0, 1, 1), (0, 1, 0, 0)), ((1, 0, 1, 0), (1, 1, 0, 0)))
FLIP_BITS = sum(FLIPS[x][y][z] << (x * 8 + y * 4 + z) for x in range(2) for y in range(2) for z in range(4))
PLANE = ((1, 0, 0), (0, 1, 0), (1, 1, 0))
LINE = ((0, 0, 2), (0, 0, 1), (0, 0, 3))


def pairs(move):
    if move is None:
        return [(i, i ^ 1) for i in range(32)]
    found = []
    for i in range(32):
        x, y, z, core = i >> 1 & 1, i >> 2 & 1, i >> 3, i & 1
        kind = core ^ FLIPS[x][y][z]
        x, y, z = x ^ move[0], y ^ move[1], z ^ move[2]
        found.append((i, ((z * 2 + y) * 2 + x) * 2 + (kind ^ FLIPS[x][y][z])))
    return found


def swap(value, move):
    return lax.ppermute(value, BOTH, pairs(move))


def place():
    aux, occ = lax.axis_index("aux"), lax.axis_index("occ")
    return occ // 2, aux % 2, aux // 2, occ % 2


def product_kernel(pattern_hbm, ground_hbm, response_hbm, away_ref, stay_ref, ground, response, pattern, product, sems):
    nbasis = ground.shape[1]
    nblocks = pattern.shape[0]
    blk = nbasis // nblocks
    rows, cols = nbasis // 8, nbasis // 4

    copies = (
        pltpu.make_async_copy(ground_hbm, ground, sems.at[0]),
        pltpu.make_async_copy(response_hbm, response, sems.at[1]),
        pltpu.make_async_copy(pattern_hbm, pattern, sems.at[2]),
    )
    for copy in copies:
        copy.start()
    x, y, z, core = place()
    kind = core ^ (FLIP_BITS >> (x * 8 + y * 4 + z)) & 1
    for copy in copies:
        copy.wait()
    product[...] = lax.dot_general(
        ground[...], response[...], (((0,), (0,)), ((), ())), preferred_element_type=jnp.float32
    )
    for i in range(nblocks):
        for j in range(i, nblocks):
            upper = 0.5 * pattern[i, j].astype(jnp.float32)
            lower = 0.5 * pattern[j, i].astype(jnp.float32)
            at_i, at_j = slice(i * blk, (i + 1) * blk), slice(j * blk, (j + 1) * blk)
            both = upper * product[at_i, at_j] + lower * product[at_j, at_i].T
            product[at_i, at_j] = both
            if i != j:
                product[at_j, at_i] = both.T

    lane = lax.broadcasted_iota(jnp.int32, (rows, nbasis), 1)
    even = sum(((lane >= rows * k).astype(jnp.int32) for k in range(1, 8))) & 1 == 0
    z_to = sum((lane >= cols * k).astype(jnp.int32) for k in range(1, 4))
    for turn in range(2):
        x_to = x ^ turn
        base = pl.multiple_of(2 * cols * x_to, 8)
        upper, lower = ([product[pl.ds(base + cols * c + at, rows), :] for c in range(2)] for at in (0, rows))
        for y_to in range(2):
            if y_to == 0:
                tiles = [jnp.where(even, u, pltpu.roll(d, rows, 1)) for u, d in zip(upper, lower)]
            else:
                tiles = [jnp.where(even, pltpu.roll(u, nbasis - rows, 1), d) for u, d in zip(upper, lower)]
            flips = lax.shift_right_logical(jnp.full_like(z_to, FLIP_BITS), x_to * 8 + y_to * 4 + z_to) & 1
            other = (flips ^ kind) == 0
            group = turn + 2 * (y ^ y_to)
            away_ref[group, :, :] = jnp.where(other, tiles[1], tiles[0])
            stay_ref[group, :, :] = jnp.where(other, tiles[0], tiles[1])


def split_kernel(own_ref, a_ref, b_ref, c_ref, out_ref):
    cols = own_ref.shape[1] // 4
    total = own_ref[...] + a_ref[...] + b_ref[...] + c_ref[...]
    x, y, z, core = place()
    for z_to in range(4):
        out_ref[z ^ z_to, :, :cols] = total[:, cols * z_to : cols * (z_to + 1)]


def turn_kernel(own_ref, a_ref, b_ref, c_ref, out_ref):
    rows, cols = out_ref.shape
    total = own_ref[...] + a_ref[...] + b_ref[...] + c_ref[...]
    turned = total[:, :cols].T
    out_ref[...] = jnp.concatenate([turned[:rows], turned[rows:]], axis=1)


def fast_shards(factors, response, pattern):
    nocc_dev, aux_dev, nbasis = factors.shape
    depth = nocc_dev * aux_dev
    rows, cols = nbasis // 8, nbasis // 4
    vmem = pl.BlockSpec(memory_space=pltpu.VMEM)
    params = pltpu.CompilerParams(vmem_limit_bytes=32 * 1024 * 1024)
    half = jax.ShapeDtypeStruct((4, rows, nbasis), jnp.float32)
    inputs = (pattern, factors.reshape(depth, nbasis), response.reshape(depth, nbasis))
    away, stay = pl.pallas_call(
        product_kernel,
        out_shape=(half, half),
        in_specs=[pl.BlockSpec(memory_space=pl.ANY)] * 3,
        out_specs=(vmem, vmem),
        scratch_shapes=[
            pltpu.VMEM((depth, nbasis), jnp.bfloat16),
            pltpu.VMEM((depth, nbasis), jnp.bfloat16),
            pltpu.SMEM(pattern.shape, jnp.int32),
            pltpu.VMEM((nbasis, nbasis), jnp.float32),
            pltpu.SemaphoreType.DMA((3,)),
        ],
        compiler_params=params,
    )(*(pltpu.with_memory_space_constraint(a, pltpu.HBM) for a in inputs))
    chip = stay + swap(away, None)
    plane = [swap(chip[move[0] + 2 * move[1]], move) for move in PLANE]
    line = pl.pallas_call(
        split_kernel,
        out_shape=jax.ShapeDtypeStruct((4, rows, 128), jnp.float32),
        in_specs=[vmem] * 4,
        out_specs=vmem,
        compiler_params=params,
    )(chip[0], *plane)
    last = [swap(line[move[2]], move) for move in LINE]
    return pl.pallas_call(
        turn_kernel,
        out_shape=jax.ShapeDtypeStruct((rows, cols), jnp.float32),
        in_specs=[vmem] * 4,
        out_specs=vmem,
        compiler_params=params,
    )(line[0], *last)


def any_shards(factors, response, pattern):
    nocc_dev, aux_dev, nbasis = factors.shape
    ground_rows = factors.reshape(nocc_dev * aux_dev, nbasis)
    response_rows = response.reshape(nocc_dev * aux_dev, nbasis)
    blk = nbasis // pattern.shape[0]
    own_cols = nbasis // lax.axis_size("occ")
    cross = lax.dot_general(
        ground_rows, response_rows, (((0,), (0,)), ((), ())), preferred_element_type=jnp.float32
    )
    masked = jnp.repeat(jnp.repeat(pattern.astype(jnp.float32), blk, axis=0), blk, axis=1) * cross
    both = 0.5 * (masked + masked.T)
    own_rows = lax.psum_scatter(both, "aux", scatter_dimension=0, tiled=True)
    summed = lax.psum(own_rows, "occ")
    return lax.dynamic_slice_in_dim(summed, lax.axis_index("occ") * own_cols, own_cols, 1)


def solution(mesh):
    in_specs = (P("occ", "aux", None), P("occ", "aux", None), P())
    out_specs = P("aux", "occ")
    sizes = dict(mesh.shape)
    shards = fast_shards if sizes["aux"] == 8 and sizes["occ"] == 4 else any_shards
    return jax.shard_map(shards, mesh=mesh, in_specs=in_specs, out_specs=out_specs, check_vma=False)
```

```python
import functools

import jax
import jax.numpy as jnp
from jax import lax
from jax.experimental import pallas as pl
from jax.experimental.pallas import tpu as pltpu
from jax.sharding import PartitionSpec as P

BOTH = ("aux", "occ")
FLIPS = (((0, 1, 1, 1), (0, 1, 0, 0)), ((0, 0, 1, 0), (1, 1, 0, 0)))
FLIP_BITS = sum(FLIPS[x][y][z] << (x * 8 + y * 4 + z) for x in range(2) for y in range(2) for z in range(4))
PLANE = ((1, 0, 0), (1, 1, 0))
LINE = ((0, 0, 1), (0, 0, 2), (0, 0, 3))


def pairs(move):
    if move is None:
        return [(i, i ^ 1) for i in range(32)]
    found = []
    for i in range(32):
        x, y, z, core = i >> 1 & 1, i >> 2 & 1, i >> 3, i & 1
        kind = core ^ FLIPS[x][y][z]
        x, y, z = x ^ move[0], y ^ move[1], z ^ move[2]
        found.append((i, ((z * 2 + y) * 2 + x) * 2 + (kind ^ FLIPS[x][y][z])))
    return found


def swap(value, move):
    return lax.ppermute(value, BOTH, pairs(move))


def place():
    aux, occ = lax.axis_index("aux"), lax.axis_index("occ")
    return occ // 2, aux % 2, aux // 2, occ % 2


def product_kernel(pattern_hbm, ground_hbm, response_hbm, out_ref, ground, response, pattern, product, whole, turned, sems):
    nbasis = ground.shape[1]
    nblocks = pattern.shape[0]
    blk = nbasis // nblocks
    rows, cols = nbasis // 8, nbasis // 4

    copies = (
        pltpu.make_async_copy(ground_hbm, ground, sems.at[0]),
        pltpu.make_async_copy(response_hbm, response, sems.at[1]),
        pltpu.make_async_copy(pattern_hbm, pattern, sems.at[2]),
    )
    for copy in copies:
        copy.start()
    x, y, z, core = place()
    kind = core ^ (FLIP_BITS >> (x * 8 + y * 4 + z)) & 1
    copies[0].wait()
    turned[...] = ground[...].T
    copies[1].wait()
    copies[2].wait()
    block = lax.dot_general(turned[0:128, :], response[...], (((1,), (0,)), ((), ())), preferred_element_type=jnp.float32)
    for j in range(3):
        product[0:128, 128 * j : 128 * j + 128] = 0.5 * pattern[0, j].astype(jnp.float32) * block[:, 128 * j : 128 * j + 128]
    block = lax.dot_general(turned[128:256, :], response[...], (((1,), (0,)), ((), ())), preferred_element_type=jnp.float32)
    for j in range(3):
        product[128:256, 128 * j : 128 * j + 128] = 0.5 * pattern[1, j].astype(jnp.float32) * block[:, 128 * j : 128 * j + 128]
    block = lax.dot_general(turned[256:384, :], response[...], (((1,), (0,)), ((), ())), preferred_element_type=jnp.float32)
    for j in range(3):
        product[256:384, 128 * j : 128 * j + 128] = 0.5 * pattern[2, j].astype(jnp.float32) * block[:, 128 * j : 128 * j + 128]
    for i in range(nblocks):
        for j in range(nblocks):
            at_i, at_j = slice(i * blk, (i + 1) * blk), slice(j * blk, (j + 1) * blk)
            whole[at_i, at_j] = product[at_i, at_j] + product[at_j, at_i].T

    lane = lax.broadcasted_iota(jnp.int32, (rows, nbasis), 1)
    even = sum(((lane >= rows * k).astype(jnp.int32) for k in range(1, 8))) & 1 == 0
    z_to = sum((lane >= cols * k).astype(jnp.int32) for k in range(1, 4))
    for turn in range(2):
        x_to = x ^ turn
        base = pl.multiple_of(2 * cols * x_to, 8)
        upper, lower = ([whole[pl.ds(base + cols * c + at, rows), :] for c in range(2)] for at in (0, rows))
        for y_to in range(2):
            if y_to == 0:
                tiles = [jnp.where(even, u, pltpu.roll(d, rows, 1)) for u, d in zip(upper, lower)]
            else:
                tiles = [jnp.where(even, pltpu.roll(u, nbasis - rows, 1), d) for u, d in zip(upper, lower)]
            flips = lax.shift_right_logical(jnp.full_like(z_to, FLIP_BITS), x_to * 8 + y_to * 4 + z_to) & 1
            other = (flips ^ kind) == 0
            stay, away = ((0, 6), (1, 6)) if turn == 0 else ((2, 1), (4, 1))
            out_ref[stay[0] + stay[1] * (y ^ y_to), :, :] = jnp.where(other, tiles[0], tiles[1])
            out_ref[away[0] + away[1] * (y ^ y_to), :, :] = jnp.where(other, tiles[1], tiles[0])


def side_kernel(own_ref, came_ref, x_ref, y_ref):
    x_ref[...] = own_ref[0] + came_ref[0]
    y_ref[...] = own_ref[1] + came_ref[1]


def split_kernel(own_ref, a_ref, b_ref, c_ref, out_ref):
    cols = own_ref.shape[1] // 4
    total = own_ref[...] + a_ref[...] + b_ref[...] + c_ref[...]
    x, y, z, core = place()
    for z_to in range(4):
        out_ref[z ^ z_to, :, :cols] = total[:, cols * z_to : cols * (z_to + 1)]


def turn_kernel(own_ref, a_ref, b_ref, c_ref, out_ref):
    rows, cols = out_ref.shape
    total = own_ref[...] + a_ref[...] + b_ref[...] + c_ref[...]
    turned = total[:, :cols].T
    out_ref[...] = jnp.concatenate([turned[:rows], turned[rows:]], axis=1)


def fast_shards(factors, response, pattern):
    nocc_dev, aux_dev, nbasis = factors.shape
    depth = nocc_dev * aux_dev
    rows, cols = nbasis // 8, nbasis // 4
    vmem = pl.BlockSpec(memory_space=pltpu.VMEM)
    params = pltpu.CompilerParams(vmem_limit_bytes=32 * 1024 * 1024)
    inputs = (pattern, factors.reshape(depth, nbasis), response.reshape(depth, nbasis))
    parts = pl.pallas_call(
        product_kernel,
        out_shape=jax.ShapeDtypeStruct((8, rows, nbasis), jnp.float32),
        in_specs=[pl.BlockSpec(memory_space=pl.ANY)] * 3,
        out_specs=vmem,
        scratch_shapes=[
            pltpu.VMEM((depth, nbasis), jnp.bfloat16),
            pltpu.VMEM((depth, nbasis), jnp.bfloat16),
            pltpu.SMEM(pattern.shape, jnp.int32),
            pltpu.VMEM((nbasis, nbasis), jnp.float32),
            pltpu.VMEM((nbasis, nbasis), jnp.float32),
            pltpu.VMEM((nbasis, depth), jnp.bfloat16),
            pltpu.SemaphoreType.DMA((3,)),
        ],
        compiler_params=params,
    )(*(pltpu.with_memory_space_constraint(a, pltpu.HBM) for a in inputs))
    side = jax.ShapeDtypeStruct((rows, nbasis), jnp.float32)
    sides = pl.pallas_call(
        side_kernel,
        out_shape=(side, side),
        in_specs=[vmem] * 2,
        out_specs=(vmem, vmem),
        cost_estimate=pl.CostEstimate(flops=100000, bytes_accessed=600000, transcendentals=0),
        compiler_params=params,
    )(parts[2:4], swap(parts[4:6], None))
    far = swap(parts[6:8], (0, 1, 0))
    near = [swap(sides[move[1]], move) for move in PLANE]
    own = parts[0:2] + far
    plane = [swap(own[1], None), *near]
    line = pl.pallas_call(
        split_kernel,
        out_shape=jax.ShapeDtypeStruct((4, rows, 128), jnp.float32),
        in_specs=[vmem] * 4,
        out_specs=vmem,
        compiler_params=params,
    )(own[0], *plane)
    last = [swap(line[move[2]], move) for move in LINE]
    return pl.pallas_call(
        turn_kernel,
        out_shape=jax.ShapeDtypeStruct((rows, cols), jnp.float32),
        in_specs=[vmem] * 4,
        out_specs=vmem,
        compiler_params=params,
    )(line[0], *last)


def any_shards(factors, response, pattern):
    nocc_dev, aux_dev, nbasis = factors.shape
    ground_rows = factors.reshape(nocc_dev * aux_dev, nbasis)
    response_rows = response.reshape(nocc_dev * aux_dev, nbasis)
    blk = nbasis // pattern.shape[0]
    own_cols = nbasis // lax.axis_size("occ")
    cross = lax.dot_general(
        ground_rows, response_rows, (((0,), (0,)), ((), ())), preferred_element_type=jnp.float32
    )
    masked = jnp.repeat(jnp.repeat(pattern.astype(jnp.float32), blk, axis=0), blk, axis=1) * cross
    both = 0.5 * (masked + masked.T)
    own_rows = lax.psum_scatter(both, "aux", scatter_dimension=0, tiled=True)
    summed = lax.psum(own_rows, "occ")
    return lax.dynamic_slice_in_dim(summed, lax.axis_index("occ") * own_cols, own_cols, 1)


def solution(mesh):
    in_specs = (P("occ", "aux", None), P("occ", "aux", None), P())
    out_specs = P("aux", "occ")
    sizes = dict(mesh.shape)
    shards = fast_shards if sizes["aux"] == 8 and sizes["occ"] == 4 else any_shards
    return jax.shard_map(shards, mesh=mesh, in_specs=in_specs, out_specs=out_specs, check_vma=False)
```

```python
import functools

import jax
import jax.numpy as jnp
from jax import lax
from jax.experimental import pallas as pl
from jax.experimental.pallas import tpu as pltpu
from jax.sharding import PartitionSpec as P

BOTH = ("aux", "occ")
FLIPS = (((0, 1, 1, 1), (0, 1, 0, 0)), ((0, 0, 1, 0), (1, 1, 1, 0)))
FLIP_BITS = sum(FLIPS[x][y][z] << (x * 8 + y * 4 + z) for x in range(2) for y in range(2) for z in range(4))
PLANE = ((1, 0, 0), (1, 1, 0))
LINE = ((0, 0, 1), (0, 0, 2), (0, 0, 3))


def pairs(move):
    if move is None:
        return [(i, i ^ 1) for i in range(32)]
    found = []
    for i in range(32):
        x, y, z, core = i >> 1 & 1, i >> 2 & 1, i >> 3, i & 1
        kind = core ^ FLIPS[x][y][z]
        x, y, z = x ^ move[0], y ^ move[1], z ^ move[2]
        found.append((i, ((z * 2 + y) * 2 + x) * 2 + (kind ^ FLIPS[x][y][z])))
    return found


def swap(value, move):
    return lax.ppermute(value, BOTH, pairs(move))


def place():
    aux, occ = lax.axis_index("aux"), lax.axis_index("occ")
    return occ // 2, aux % 2, aux // 2, occ % 2


def product_kernel(pattern_hbm, ground_hbm, response_hbm, out_ref, ground, response, pattern, product, whole, turned, sems):
    nbasis = ground.shape[1]
    nblocks = pattern.shape[0]
    blk = nbasis // nblocks
    rows, cols = nbasis // 8, nbasis // 4

    step = ground.shape[0] // 1
    parts = [pl.ds(k * step, step) for k in range(1)]
    firsts = [pltpu.make_async_copy(ground_hbm.at[here], ground.at[here], sems.at[3 + k]) for k, here in enumerate(parts)]
    second = pltpu.make_async_copy(response_hbm, response, sems.at[0])
    masks = pltpu.make_async_copy(pattern_hbm, pattern, sems.at[1])
    for first in firsts:
        first.start()
    second.start()
    masks.start()
    x, y, z, core = place()
    kind = core ^ (FLIP_BITS >> (x * 8 + y * 4 + z)) & 1
    for first, here in zip(firsts, parts):
        first.wait()
        turned[:, here] = ground[here, :].T
    second.wait()
    masks.wait()
    block = lax.dot_general(turned[0:128, :], response[...], (((1,), (0,)), ((), ())), preferred_element_type=jnp.float32)
    for j in range(3):
        product[0:128, 128 * j : 128 * j + 128] = 0.5 * pattern[0, j].astype(jnp.float32) * block[:, 128 * j : 128 * j + 128]
    block = lax.dot_general(turned[128:256, :], response[...], (((1,), (0,)), ((), ())), preferred_element_type=jnp.float32)
    for j in range(3):
        product[128:256, 128 * j : 128 * j + 128] = 0.5 * pattern[1, j].astype(jnp.float32) * block[:, 128 * j : 128 * j + 128]
    block = lax.dot_general(turned[256:384, :], response[...], (((1,), (0,)), ((), ())), preferred_element_type=jnp.float32)
    for j in range(3):
        product[256:384, 128 * j : 128 * j + 128] = 0.5 * pattern[2, j].astype(jnp.float32) * block[:, 128 * j : 128 * j + 128]
    for i in range(nblocks):
        for j in range(nblocks):
            at_i, at_j = slice(i * blk, (i + 1) * blk), slice(j * blk, (j + 1) * blk)
            whole[at_i, at_j] = product[at_i, at_j] + product[at_j, at_i].T

    lane = lax.broadcasted_iota(jnp.int32, (rows, nbasis), 1)
    even = sum(((lane >= rows * k).astype(jnp.int32) for k in range(1, 8))) & 1 == 0
    z_to = sum((lane >= cols * k).astype(jnp.int32) for k in range(1, 4))
    for x_to in range(2):
        turn = x ^ x_to
        base = 2 * cols * x_to
        upper, lower = ([whole[base + cols * c + at : base + cols * c + at + rows, :] for c in range(2)] for at in (0, rows))
        for y_to in range(2):
            if y_to == 0:
                tiles = [jnp.where(even, u, pltpu.roll(d, rows, 1)) for u, d in zip(upper, lower)]
            else:
                tiles = [jnp.where(even, pltpu.roll(u, nbasis - rows, 1), d) for u, d in zip(upper, lower)]
            flips = lax.shift_right_logical(jnp.full_like(z_to, FLIP_BITS), x_to * 8 + y_to * 4 + z_to) & 1
            other = (flips ^ kind) == 0
            step = y ^ y_to
            out_ref[turn * (2 + step) + (1 - turn) * 6 * step, :, :] = jnp.where(other, tiles[0], tiles[1])
            out_ref[turn * (4 + step) + (1 - turn) * (1 + 6 * step), :, :] = jnp.where(other, tiles[1], tiles[0])


def side_kernel(own_ref, came_ref, x_ref, y_ref):
    x_ref[...] = own_ref[0] + came_ref[0]
    y_ref[...] = own_ref[1] + came_ref[1]


def split_kernel(own_ref, a_ref, b_ref, c_ref, out_ref):
    cols = own_ref.shape[1] // 4
    total = own_ref[...] + a_ref[...] + b_ref[...] + c_ref[...]
    x, y, z, core = place()
    for z_to in range(4):
        out_ref[z ^ z_to, :, :cols] = total[:, cols * z_to : cols * (z_to + 1)]


def turn_kernel(own_ref, a_ref, b_ref, c_ref, out_ref):
    rows, cols = out_ref.shape
    total = own_ref[...] + a_ref[...] + b_ref[...] + c_ref[...]
    turned = total[:, :cols].T
    out_ref[...] = jnp.concatenate([turned[:rows], turned[rows:]], axis=1)


def fast_shards(factors, response, pattern):
    nocc_dev, aux_dev, nbasis = factors.shape
    depth = nocc_dev * aux_dev
    rows, cols = nbasis // 8, nbasis // 4
    vmem = pl.BlockSpec(memory_space=pltpu.VMEM)
    params = pltpu.CompilerParams(vmem_limit_bytes=32 * 1024 * 1024)
    inputs = (pattern, factors.reshape(depth, nbasis), response.reshape(depth, nbasis))
    parts = pl.pallas_call(
        product_kernel,
        out_shape=jax.ShapeDtypeStruct((8, rows, nbasis), jnp.float32),
        in_specs=[pl.BlockSpec(memory_space=pl.ANY)] * 3,
        out_specs=vmem,
        scratch_shapes=[
            pltpu.VMEM((depth, nbasis), jnp.bfloat16),
            pltpu.VMEM((depth, nbasis), jnp.bfloat16),
            pltpu.SMEM(pattern.shape, jnp.int32),
            pltpu.VMEM((nbasis, nbasis), jnp.float32),
            pltpu.VMEM((nbasis, nbasis), jnp.float32),
            pltpu.VMEM((nbasis, depth), jnp.bfloat16),
            pltpu.SemaphoreType.DMA((4,)),
        ],
        compiler_params=params,
    )(*(pltpu.with_memory_space_constraint(a, pltpu.HBM) for a in inputs))
    side = jax.ShapeDtypeStruct((rows, nbasis), jnp.float32)
    sides = pl.pallas_call(
        side_kernel,
        out_shape=(side, side),
        in_specs=[vmem] * 2,
        out_specs=(vmem, vmem),
        cost_estimate=pl.CostEstimate(flops=100000, bytes_accessed=600000, transcendentals=0),
        compiler_params=params,
    )(parts[2:4], swap(parts[4:6], None))
    far = swap(parts[6:8], (0, 1, 0))
    near = [swap(sides[move[1]], move) for move in PLANE]
    own = parts[0:2] + far
    plane = [swap(own[1], None), *near]
    line = pl.pallas_call(
        split_kernel,
        out_shape=jax.ShapeDtypeStruct((4, rows, 128), jnp.float32),
        in_specs=[vmem] * 4,
        out_specs=vmem,
        compiler_params=params,
    )(own[0], *plane)
    last = [swap(line[move[2]], move) for move in LINE]
    return pl.pallas_call(
        turn_kernel,
        out_shape=jax.ShapeDtypeStruct((rows, cols), jnp.float32),
        in_specs=[vmem] * 4,
        out_specs=vmem,
        compiler_params=params,
    )(line[0], *last)


def any_shards(factors, response, pattern):
    nocc_dev, aux_dev, nbasis = factors.shape
    ground_rows = factors.reshape(nocc_dev * aux_dev, nbasis)
    response_rows = response.reshape(nocc_dev * aux_dev, nbasis)
    blk = nbasis // pattern.shape[0]
    own_cols = nbasis // lax.axis_size("occ")
    cross = lax.dot_general(
        ground_rows, response_rows, (((0,), (0,)), ((), ())), preferred_element_type=jnp.float32
    )
    masked = jnp.repeat(jnp.repeat(pattern.astype(jnp.float32), blk, axis=0), blk, axis=1) * cross
    both = 0.5 * (masked + masked.T)
    own_rows = lax.psum_scatter(both, "aux", scatter_dimension=0, tiled=True)
    summed = lax.psum(own_rows, "occ")
    return lax.dynamic_slice_in_dim(summed, lax.axis_index("occ") * own_cols, own_cols, 1)


def solution(mesh):
    in_specs = (P("occ", "aux", None), P("occ", "aux", None), P())
    out_specs = P("aux", "occ")
    sizes = dict(mesh.shape)
    shards = fast_shards if sizes["aux"] == 8 and sizes["occ"] == 4 else any_shards
    return jax.shard_map(shards, mesh=mesh, in_specs=in_specs, out_specs=out_specs, check_vma=False)
```

```python
import jax
import jax.numpy as jnp
from jax import lax
from jax.experimental import pallas as pl
from jax.experimental.pallas import tpu as pltpu
from jax.sharding import PartitionSpec as P

BOTH = ("aux", "occ")
FLIPS = (((1, 1, 0, 1), (0, 1, 1, 1)), ((0, 0, 1, 0), (0, 0, 0, 1)))
FLIP_BITS = sum(FLIPS[x][y][z] << (x * 8 + y * 4 + z) for x in range(2) for y in range(2) for z in range(4))
PLANE = ((1, 0, 0), (1, 1, 0))
FIRST = (0, 1, 0)
NEAR = (0, 0, 1)
FAR = ((0, 0, 3), (0, 0, 2))


def pairs(moves):
    if not moves:
        return [(i, i ^ 1) for i in range(32)]
    found = []
    for i in range(32):
        x, y, z, core = i >> 1 & 1, i >> 2 & 1, i >> 3, i & 1
        kind = core ^ FLIPS[x][y][z]
        move = moves[kind]
        x, y, z = x ^ move[0], y ^ move[1], z ^ move[2]
        found.append((i, ((z * 2 + y) * 2 + x) * 2 + (kind ^ FLIPS[x][y][z])))
    return found


def swap(value, *moves):
    return lax.ppermute(value, BOTH, pairs(moves))


def place():
    aux, occ = lax.axis_index("aux"), lax.axis_index("occ")
    return occ // 2, aux % 2, aux // 2, occ % 2


def product_kernel(pattern_hbm, ground_hbm, response_hbm, out_ref, ground, response, pattern, product, whole, turned, sems):
    nbasis = ground.shape[1]
    nblocks = pattern.shape[0]
    blk = nbasis // nblocks
    rows, cols = nbasis // 8, nbasis // 4

    step = ground.shape[0] // 1
    parts = [pl.ds(k * step, step) for k in range(1)]
    firsts = [pltpu.make_async_copy(ground_hbm.at[here], ground.at[here], sems.at[3 + k]) for k, here in enumerate(parts)]
    second = pltpu.make_async_copy(response_hbm, response, sems.at[0])
    masks = pltpu.make_async_copy(pattern_hbm, pattern, sems.at[1])
    for first in firsts:
        first.start()
    second.start()
    masks.start()
    x, y, z, core = place()
    kind = core ^ (FLIP_BITS >> (x * 8 + y * 4 + z)) & 1
    for first, here in zip(firsts, parts):
        first.wait()
        turned[:, here] = ground[here, :].T
    second.wait()
    masks.wait()
    block = lax.dot_general(turned[0:128, :], response[...], (((1,), (0,)), ((), ())), preferred_element_type=jnp.float32)
    for j in range(3):
        product[0:128, 128 * j : 128 * j + 128] = 0.5 * pattern[0, j].astype(jnp.float32) * block[:, 128 * j : 128 * j + 128]
    block = lax.dot_general(turned[128:256, :], response[...], (((1,), (0,)), ((), ())), preferred_element_type=jnp.float32)
    for j in range(3):
        product[128:256, 128 * j : 128 * j + 128] = 0.5 * pattern[1, j].astype(jnp.float32) * block[:, 128 * j : 128 * j + 128]
    block = lax.dot_general(turned[256:384, :], response[...], (((1,), (0,)), ((), ())), preferred_element_type=jnp.float32)
    for j in range(3):
        product[256:384, 128 * j : 128 * j + 128] = 0.5 * pattern[2, j].astype(jnp.float32) * block[:, 128 * j : 128 * j + 128]
    for i in range(nblocks):
        for j in range(nblocks):
            at_i, at_j = slice(i * blk, (i + 1) * blk), slice(j * blk, (j + 1) * blk)
            whole[at_i, at_j] = product[at_i, at_j] + product[at_j, at_i].T

    lane = lax.broadcasted_iota(jnp.int32, (8, nbasis), 1)
    even = sum((lane >= rows * k).astype(jnp.int32) for k in range(1, 8)) & 1 == 0
    z_to = sum((lane >= cols * k).astype(jnp.int32) for k in range(1, 4))
    left, two, three = z_to & 1 == 0, z_to == z ^ 2, z_to == z ^ 3
    mine = jnp.full_like(lane, kind) == 0

    def cut(at):
        return whole[at : at + rows, :].reshape(rows // 8, 8, nbasis)

    for x_to in range(2):
        turn = x ^ x_to
        upper, lower = ([cut(cols * (2 * x_to + c) + at) for c in range(2)] for at in (0, rows))
        for y_to in range(2):
            if y_to == 0:
                tiles = [jnp.where(even, u, pltpu.roll(d, rows, 2)) for u, d in zip(upper, lower)]
            else:
                tiles = [jnp.where(even, pltpu.roll(u, nbasis - rows, 2), d) for u, d in zip(upper, lower)]
            flips = lax.shift_right_logical(jnp.full_like(z_to, FLIP_BITS), x_to * 8 + y_to * 4 + z_to) & 1 == 0
            zero, one = jnp.where(flips, tiles[0], tiles[1]), jnp.where(flips, tiles[1], tiles[0])
            moved = jnp.where(three, one, zero)
            moved = jnp.where(left, pltpu.roll(moved, nbasis - cols, 2), pltpu.roll(moved, cols, 2))
            zero, one = jnp.where(two, moved, zero), jnp.where(three, moved, one)
            step = y ^ y_to
            own, other = jnp.where(mine, zero, one), jnp.where(mine, one, zero)
            out_ref[turn * (2 + step) + (1 - turn) * 6 * step, :, :] = own.reshape(rows, nbasis)
            out_ref[turn * (4 + step) + (1 - turn) * (1 + 6 * step), :, :] = other.reshape(rows, nbasis)


def side_kernel(own_ref, came_ref, x_ref, y_ref):
    x_ref[...] = own_ref[0] + came_ref[0]
    y_ref[...] = own_ref[1] + came_ref[1]


def split_kernel(own_ref, a_ref, b_ref, c_ref, out_ref):
    cols = own_ref.shape[1] // 4
    total = own_ref[...] + a_ref[...] + b_ref[...] + c_ref[...]
    x, y, z, core = place()
    kind = core ^ (FLIP_BITS >> (x * 8 + y * 4 + z)) & 1
    for z_to in range(4):
        turn = z ^ z_to
        slot = jnp.where((turn >= 2) & (kind == 0), 5 - turn, turn)
        out_ref[slot, :, :cols] = total[:, cols * z_to : cols * (z_to + 1)]


def turn_kernel(own_ref, a_ref, b_ref, c_ref, out_ref):
    rows, cols = out_ref.shape
    total = own_ref[...] + a_ref[...] + b_ref[...] + c_ref[...]
    turned = total[:, :cols].T
    out_ref[...] = jnp.concatenate([turned[:rows], turned[rows:]], axis=1)


def fast_shards(factors, response, pattern):
    nocc_dev, aux_dev, nbasis = factors.shape
    depth = nocc_dev * aux_dev
    rows, cols = nbasis // 8, nbasis // 4
    vmem = pl.BlockSpec(memory_space=pltpu.VMEM)
    params = pltpu.CompilerParams(vmem_limit_bytes=32 * 1024 * 1024)
    inputs = (pattern, factors.reshape(depth, nbasis), response.reshape(depth, nbasis))
    parts = pl.pallas_call(
        product_kernel,
        out_shape=jax.ShapeDtypeStruct((8, rows, nbasis), jnp.float32),
        in_specs=[pl.BlockSpec(memory_space=pl.ANY)] * 3,
        out_specs=vmem,
        scratch_shapes=[
            pltpu.VMEM((depth, nbasis), jnp.bfloat16),
            pltpu.VMEM((depth, nbasis), jnp.bfloat16),
            pltpu.SMEM(pattern.shape, jnp.int32),
            pltpu.VMEM((nbasis, nbasis), jnp.float32),
            pltpu.VMEM((nbasis, nbasis), jnp.float32),
            pltpu.VMEM((nbasis, depth), jnp.bfloat16),
            pltpu.SemaphoreType.DMA((4,)),
        ],
        compiler_params=params,
    )(*(pltpu.with_memory_space_constraint(a, pltpu.HBM) for a in inputs))
    side = jax.ShapeDtypeStruct((rows, nbasis), jnp.float32)
    sides = pl.pallas_call(
        side_kernel,
        out_shape=(side, side),
        in_specs=[vmem] * 2,
        out_specs=(vmem, vmem),
        cost_estimate=pl.CostEstimate(flops=100000, bytes_accessed=600000, transcendentals=0),
        compiler_params=params,
    )(parts[2:4], swap(parts[4:6]))
    first = swap(parts[6:8], FIRST, FIRST)
    near = [swap(sides[move[1]], move, move) for move in PLANE]
    own = parts[0:2] + first
    plane = [swap(own[1]), *near]
    line = pl.pallas_call(
        split_kernel,
        out_shape=jax.ShapeDtypeStruct((4, rows, 128), jnp.float32),
        in_specs=[vmem] * 4,
        out_specs=vmem,
        compiler_params=params,
    )(own[0], *plane)
    far = swap(line[2:], *FAR)
    last = [swap(line[1], NEAR, NEAR), swap(far[1]), far[0]]
    return pl.pallas_call(
        turn_kernel,
        out_shape=jax.ShapeDtypeStruct((rows, cols), jnp.float32),
        in_specs=[vmem] * 4,
        out_specs=vmem,
        compiler_params=params,
    )(line[0], *last)


def any_shards(factors, response, pattern):
    nocc_dev, aux_dev, nbasis = factors.shape
    ground_rows = factors.reshape(nocc_dev * aux_dev, nbasis)
    response_rows = response.reshape(nocc_dev * aux_dev, nbasis)
    blk = nbasis // pattern.shape[0]
    own_cols = nbasis // lax.axis_size("occ")
    cross = lax.dot_general(
        ground_rows, response_rows, (((0,), (0,)), ((), ())), preferred_element_type=jnp.float32
    )
    masked = jnp.repeat(jnp.repeat(pattern.astype(jnp.float32), blk, axis=0), blk, axis=1) * cross
    both = 0.5 * (masked + masked.T)
    own_rows = lax.psum_scatter(both, "aux", scatter_dimension=0, tiled=True)
    summed = lax.psum(own_rows, "occ")
    return lax.dynamic_slice_in_dim(summed, lax.axis_index("occ") * own_cols, own_cols, 1)


def solution(mesh):
    in_specs = (P("occ", "aux", None), P("occ", "aux", None), P())
    out_specs = P("aux", "occ")
    sizes = dict(mesh.shape)
    shards = fast_shards if sizes["aux"] == 8 and sizes["occ"] == 4 else any_shards
    return jax.shard_map(shards, mesh=mesh, in_specs=in_specs, out_specs=out_specs, check_vma=False)
```

```python
import jax
import jax.numpy as jnp
from jax import lax
from jax.experimental import pallas as pl
from jax.experimental.pallas import tpu as pltpu
from jax.sharding import PartitionSpec as P

BOTH = ("aux", "occ")
FLIPS = (((1, 1, 0, 1), (1, 1, 0, 1)), ((0, 0, 1, 0), (0, 0, 0, 0)))
FLIP_BITS = sum(FLIPS[x][y][z] << (x * 8 + y * 4 + z) for x in range(2) for y in range(2) for z in range(4))
PLANE = ((1, 0, 0), (1, 1, 0))
FIRST = (0, 1, 0)
NEAR = (0, 0, 1)
FAR = ((0, 0, 3), (0, 0, 2))


def pairs(moves):
    if not moves:
        return [(i, i ^ 1) for i in range(32)]
    found = []
    for i in range(32):
        x, y, z, core = i >> 1 & 1, i >> 2 & 1, i >> 3, i & 1
        kind = core ^ FLIPS[x][y][z]
        move = moves[kind]
        x, y, z = x ^ move[0], y ^ move[1], z ^ move[2]
        found.append((i, ((z * 2 + y) * 2 + x) * 2 + (kind ^ FLIPS[x][y][z])))
    return found


def swap(value, *moves):
    return lax.ppermute(value, BOTH, pairs(moves))


def place():
    aux, occ = lax.axis_index("aux"), lax.axis_index("occ")
    return occ // 2, aux % 2, aux // 2, occ % 2


def product_kernel(pattern_hbm, ground_hbm, response_hbm, out_ref, ground, response, pattern, product, whole, turned, sems):
    nbasis = ground.shape[1]
    nblocks = pattern.shape[0]
    blk = nbasis // nblocks
    rows, cols = nbasis // 8, nbasis // 4

    first = pltpu.make_async_copy(ground_hbm, ground, sems.at[0])
    second = pltpu.make_async_copy(response_hbm, response, sems.at[1])
    masks = pltpu.make_async_copy(pattern_hbm, pattern, sems.at[2])
    first.start()
    second.start()
    masks.start()
    x, y, z, core = place()
    kind = core ^ (FLIP_BITS >> (x * 8 + y * 4 + z)) & 1
    first.wait()
    turned[...] = ground[...].T
    second.wait()
    masks.wait()
    for i in range(nblocks):
        at_i = slice(i * blk, (i + 1) * blk)
        block = lax.dot_general(
            turned[at_i, :], response[...], (((1,), (0,)), ((), ())), preferred_element_type=jnp.float32
        )
        for j in range(nblocks):
            at_j = slice(j * blk, (j + 1) * blk)
            product[at_i, at_j] = 0.5 * pattern[i, j].astype(jnp.float32) * block[:, at_j]
    for i in range(nblocks):
        for j in range(nblocks):
            at_i, at_j = slice(i * blk, (i + 1) * blk), slice(j * blk, (j + 1) * blk)
            whole[at_i, at_j] = product[at_i, at_j] + product[at_j, at_i].T

    lane = lax.broadcasted_iota(jnp.int32, (8, nbasis), 1)
    even = sum((lane >= rows * k).astype(jnp.int32) for k in range(1, 8)) & 1 == 0
    z_to = sum((lane >= cols * k).astype(jnp.int32) for k in range(1, 4))
    left, two, three = z_to & 1 == 0, z_to == z ^ 2, z_to == z ^ 3
    mine = jnp.full_like(lane, kind) == 0

    def cut(at):
        return whole[at : at + rows, :].reshape(rows // 8, 8, nbasis)

    for x_to in range(2):
        turn = x ^ x_to
        upper, lower = ([cut(cols * (2 * x_to + c) + at) for c in range(2)] for at in (0, rows))
        for y_to in range(2):
            if y_to == 0:
                tiles = [jnp.where(even, u, pltpu.roll(d, rows, 2)) for u, d in zip(upper, lower)]
            else:
                tiles = [jnp.where(even, pltpu.roll(u, nbasis - rows, 2), d) for u, d in zip(upper, lower)]
            flips = lax.shift_right_logical(jnp.full_like(z_to, FLIP_BITS), x_to * 8 + y_to * 4 + z_to) & 1 == 0
            zero, one = jnp.where(flips, tiles[0], tiles[1]), jnp.where(flips, tiles[1], tiles[0])
            moved = jnp.where(three, one, zero)
            moved = jnp.where(left, pltpu.roll(moved, nbasis - cols, 2), pltpu.roll(moved, cols, 2))
            zero, one = jnp.where(two, moved, zero), jnp.where(three, moved, one)
            step = y ^ y_to
            own, other = jnp.where(mine, zero, one), jnp.where(mine, one, zero)
            out_ref[turn * (2 + step) + (1 - turn) * 6 * step, :, :] = own.reshape(rows, nbasis)
            out_ref[turn * (4 + step) + (1 - turn) * (1 + 6 * step), :, :] = other.reshape(rows, nbasis)


def side_kernel(own_ref, came_ref, x_ref, y_ref):
    x_ref[...] = own_ref[0] + came_ref[0]
    y_ref[...] = own_ref[1] + came_ref[1]


def split_kernel(own_ref, a_ref, b_ref, c_ref, out_ref):
    cols = own_ref.shape[1] // 4
    total = own_ref[...] + a_ref[...] + b_ref[...] + c_ref[...]
    x, y, z, core = place()
    kind = core ^ (FLIP_BITS >> (x * 8 + y * 4 + z)) & 1
    for z_to in range(4):
        turn = z ^ z_to
        slot = jnp.where((turn >= 2) & (kind == 0), 5 - turn, turn)
        out_ref[slot, :, :cols] = total[:, cols * z_to : cols * (z_to + 1)]


def turn_kernel(own_ref, a_ref, b_ref, c_ref, out_ref):
    rows, cols = out_ref.shape
    total = own_ref[...] + a_ref[...] + b_ref[...] + c_ref[...]
    turned = total[:, :cols].T
    out_ref[...] = jnp.concatenate([turned[:rows], turned[rows:]], axis=1)


def fast_shards(factors, response, pattern):
    nocc_dev, aux_dev, nbasis = factors.shape
    depth = nocc_dev * aux_dev
    rows, cols = nbasis // 8, nbasis // 4
    vmem = pl.BlockSpec(memory_space=pltpu.VMEM)
    params = pltpu.CompilerParams(vmem_limit_bytes=32 * 1024 * 1024)
    inputs = (pattern, factors.reshape(depth, nbasis), response.reshape(depth, nbasis))
    parts = pl.pallas_call(
        product_kernel,
        out_shape=jax.ShapeDtypeStruct((8, rows, nbasis), jnp.float32),
        in_specs=[pl.BlockSpec(memory_space=pl.ANY)] * 3,
        out_specs=vmem,
        scratch_shapes=[
            pltpu.VMEM((depth, nbasis), jnp.bfloat16),
            pltpu.VMEM((depth, nbasis), jnp.bfloat16),
            pltpu.SMEM(pattern.shape, jnp.int32),
            pltpu.VMEM((nbasis, nbasis), jnp.float32),
            pltpu.VMEM((nbasis, nbasis), jnp.float32),
            pltpu.VMEM((nbasis, depth), jnp.bfloat16),
            pltpu.SemaphoreType.DMA((3,)),
        ],
        compiler_params=params,
    )(*(pltpu.with_memory_space_constraint(a, pltpu.HBM) for a in inputs))
    side = jax.ShapeDtypeStruct((rows, nbasis), jnp.float32)
    sides = pl.pallas_call(
        side_kernel,
        out_shape=(side, side),
        in_specs=[vmem] * 2,
        out_specs=(vmem, vmem),
        cost_estimate=pl.CostEstimate(flops=100000, bytes_accessed=600000, transcendentals=0),
        compiler_params=params,
    )(parts[2:4], swap(parts[4:6]))
    first = swap(parts[6:8], FIRST, FIRST)
    near = [swap(sides[move[1]], move, move) for move in PLANE]
    own = parts[0:2] + first
    plane = [swap(own[1]), *near]
    line = pl.pallas_call(
        split_kernel,
        out_shape=jax.ShapeDtypeStruct((4, rows, 128), jnp.float32),
        in_specs=[vmem] * 4,
        out_specs=vmem,
        compiler_params=params,
    )(own[0], *plane)
    far = swap(line[2:], *FAR)
    last = [swap(line[1], NEAR, NEAR), swap(far[1]), far[0]]
    return pl.pallas_call(
        turn_kernel,
        out_shape=jax.ShapeDtypeStruct((rows, cols), jnp.float32),
        in_specs=[vmem] * 4,
        out_specs=vmem,
        compiler_params=params,
    )(line[0], *last)


def any_shards(factors, response, pattern):
    nocc_dev, aux_dev, nbasis = factors.shape
    ground_rows = factors.reshape(nocc_dev * aux_dev, nbasis)
    response_rows = response.reshape(nocc_dev * aux_dev, nbasis)
    blk = nbasis // pattern.shape[0]
    own_cols = nbasis // lax.axis_size("occ")
    cross = lax.dot_general(
        ground_rows, response_rows, (((0,), (0,)), ((), ())), preferred_element_type=jnp.float32
    )
    masked = jnp.repeat(jnp.repeat(pattern.astype(jnp.float32), blk, axis=0), blk, axis=1) * cross
    both = 0.5 * (masked + masked.T)
    own_rows = lax.psum_scatter(both, "aux", scatter_dimension=0, tiled=True)
    summed = lax.psum(own_rows, "occ")
    return lax.dynamic_slice_in_dim(summed, lax.axis_index("occ") * own_cols, own_cols, 1)


def solution(mesh):
    in_specs = (P("occ", "aux", None), P("occ", "aux", None), P())
    out_specs = P("aux", "occ")
    sizes = dict(mesh.shape)
    shards = fast_shards if sizes["aux"] == 8 and sizes["occ"] == 4 else any_shards
    return jax.shard_map(shards, mesh=mesh, in_specs=in_specs, out_specs=out_specs, check_vma=False)
```

```python
import jax
import jax.numpy as jnp
from jax import lax
from jax.experimental import pallas as pl
from jax.experimental.pallas import tpu as pltpu
from jax.sharding import PartitionSpec as P

BOTH = ("aux", "occ")
FLIPS = (((1, 0, 0, 1), (1, 1, 0, 1)), ((0, 0, 1, 0), (0, 0, 0, 1)))
FLIP_BITS = sum(FLIPS[x][y][z] << (x * 8 + y * 4 + z) for x in range(2) for y in range(2) for z in range(4))
PLANE = ((1, 0, 0), (1, 1, 0))
FIRST = (0, 1, 0)
NEAR = (0, 0, 1)
FAR = ((0, 0, 3), (0, 0, 2))


def pairs(moves):
    if not moves:
        return [(i, i ^ 1) for i in range(32)]
    found = []
    for i in range(32):
        x, y, z, core = i >> 1 & 1, i >> 2 & 1, i >> 3, i & 1
        kind = core ^ FLIPS[x][y][z]
        move = moves[kind]
        x, y, z = x ^ move[0], y ^ move[1], z ^ move[2]
        found.append((i, ((z * 2 + y) * 2 + x) * 2 + (kind ^ FLIPS[x][y][z])))
    return found


def swap(value, *moves):
    return lax.ppermute(value, BOTH, pairs(moves))


def place():
    aux, occ = lax.axis_index("aux"), lax.axis_index("occ")
    return occ // 2, aux % 2, aux // 2, occ % 2


def product_kernel(pattern_hbm, ground_hbm, response_hbm, out_ref, ground, response, pattern, product, whole, turned, sems):
    nbasis = ground.shape[1]
    nblocks = pattern.shape[0]
    blk = nbasis // nblocks
    rows, cols = nbasis // 8, nbasis // 4

    first = pltpu.make_async_copy(ground_hbm, ground, sems.at[0])
    second = pltpu.make_async_copy(response_hbm, response, sems.at[1])
    masks = pltpu.make_async_copy(pattern_hbm, pattern, sems.at[2])
    first.start()
    second.start()
    masks.start()
    x, y, z, core = place()
    kind = core ^ (FLIP_BITS >> (x * 8 + y * 4 + z)) & 1
    first.wait()
    turned[...] = ground[...].T
    second.wait()
    masks.wait()
    block = lax.dot_general(turned[0:128, :], response[...], (((1,), (0,)), ((), ())), preferred_element_type=jnp.float32)
    for j in range(3):
        product[0:128, 128 * j : 128 * j + 128] = 0.5 * pattern[0, j].astype(jnp.float32) * block[:, 128 * j : 128 * j + 128]
    block = lax.dot_general(turned[128:256, :], response[...], (((1,), (0,)), ((), ())), preferred_element_type=jnp.float32)
    for j in range(3):
        product[128:256, 128 * j : 128 * j + 128] = 0.5 * pattern[1, j].astype(jnp.float32) * block[:, 128 * j : 128 * j + 128]
    block = lax.dot_general(turned[256:384, :], response[...], (((1,), (0,)), ((), ())), preferred_element_type=jnp.float32)
    for j in range(3):
        product[256:384, 128 * j : 128 * j + 128] = 0.5 * pattern[2, j].astype(jnp.float32) * block[:, 128 * j : 128 * j + 128]
    for i in range(nblocks):
        for j in range(nblocks):
            at_i, at_j = slice(i * blk, (i + 1) * blk), slice(j * blk, (j + 1) * blk)
            whole[at_i, at_j] = product[at_i, at_j] + product[at_j, at_i].T

    lane = lax.broadcasted_iota(jnp.int32, (8, nbasis), 1)
    even = sum((lane >= rows * k).astype(jnp.int32) for k in range(1, 8)) & 1 == 0
    z_to = sum((lane >= cols * k).astype(jnp.int32) for k in range(1, 4))
    left, two, three = z_to & 1 == 0, z_to == z ^ 2, z_to == z ^ 3
    mine = jnp.full_like(lane, kind) == 0

    def cut(at):
        return whole[at : at + rows, :].reshape(rows // 8, 8, nbasis)

    for x_to in range(2):
        turn = x ^ x_to
        upper, lower = ([cut(cols * (2 * x_to + c) + at) for c in range(2)] for at in (0, rows))
        for y_to in range(2):
            if y_to == 0:
                tiles = [jnp.where(even, u, pltpu.roll(d, rows, 2)) for u, d in zip(upper, lower)]
            else:
                tiles = [jnp.where(even, pltpu.roll(u, nbasis - rows, 2), d) for u, d in zip(upper, lower)]
            flips = lax.shift_right_logical(jnp.full_like(z_to, FLIP_BITS), x_to * 8 + y_to * 4 + z_to) & 1 == 0
            zero, one = jnp.where(flips, tiles[0], tiles[1]), jnp.where(flips, tiles[1], tiles[0])
            moved = jnp.where(three, one, zero)
            moved = jnp.where(left, pltpu.roll(moved, nbasis - cols, 2), pltpu.roll(moved, cols, 2))
            zero, one = jnp.where(two, moved, zero), jnp.where(three, moved, one)
            step = y ^ y_to
            own, other = jnp.where(mine, zero, one), jnp.where(mine, one, zero)
            out_ref[turn * (2 + step) + (1 - turn) * 6 * step, :, :] = own.reshape(rows, nbasis)
            out_ref[turn * (4 + step) + (1 - turn) * (1 + 6 * step), :, :] = other.reshape(rows, nbasis)


def side_kernel(own_ref, came_ref, x_ref, y_ref):
    x_ref[...] = own_ref[0] + came_ref[0]
    y_ref[...] = own_ref[1] + came_ref[1]


def split_kernel(own_ref, a_ref, b_ref, c_ref, tile_ref, far_ref):
    rows, nbasis = own_ref.shape
    cols, half = nbasis // 4, rows // 2
    total = own_ref[...] + a_ref[...] + b_ref[...] + c_ref[...]
    x, y, z, core = place()
    for z_to in range(4):
        tile_ref[jnp.minimum(z ^ z_to, 2), :, :cols] = total[:, cols * z_to : cols * (z_to + 1)]
    turned = pltpu.roll(total, nbasis // 2, 1)
    lane = lax.broadcasted_iota(jnp.int32, (half, nbasis), 1)
    low = lane < nbasis // 2
    high_far = jnp.full_like(lane, z // 2) == 0
    far_ref[...] = jnp.where(
        high_far, jnp.where(low, turned[:half], total[half:]), jnp.where(low, total[:half], turned[half:])
    )


def part_of(far_ref, parity):
    half, nbasis = far_ref.shape
    cols = nbasis // 4
    x, y, z, core = place()
    odd = jnp.full(far_ref.shape, (z ^ parity) & 1) == 1
    far = jnp.where(odd, pltpu.roll(far_ref[...], 3 * cols, 1), far_ref[...])
    return far[:, :cols], far[:, 2 * cols : 3 * cols]


def pick_kernel(far_ref, out_ref):
    half, cols = far_ref.shape[0], far_ref.shape[1] // 4
    out_ref[:half, :cols], out_ref[half:, :cols] = part_of(far_ref, 1)


def home_kernel(home_ref, far_ref, out_ref):
    half, cols = far_ref.shape[0], far_ref.shape[1] // 4
    top, bottom = part_of(far_ref, 0)
    out_ref[:half, :cols] = home_ref[:half, :cols] + top
    out_ref[half:, :cols] = home_ref[half:, :cols] + bottom


def turn_kernel(home_ref, near_ref, other_ref, out_ref):
    rows, cols = out_ref.shape
    total = home_ref[...] + near_ref[...] + other_ref[...]
    turned = total[:, :cols].T
    out_ref[...] = jnp.concatenate([turned[:rows], turned[rows:]], axis=1)


def fast_shards(factors, response, pattern):
    nocc_dev, aux_dev, nbasis = factors.shape
    depth = nocc_dev * aux_dev
    rows, cols = nbasis // 8, nbasis // 4
    vmem = pl.BlockSpec(memory_space=pltpu.VMEM)
    params = pltpu.CompilerParams(vmem_limit_bytes=32 * 1024 * 1024)
    inputs = (pattern, factors.reshape(depth, nbasis), response.reshape(depth, nbasis))
    parts = pl.pallas_call(
        product_kernel,
        out_shape=jax.ShapeDtypeStruct((8, rows, nbasis), jnp.float32),
        in_specs=[pl.BlockSpec(memory_space=pl.ANY)] * 3,
        out_specs=vmem,
        scratch_shapes=[
            pltpu.VMEM((depth, nbasis), jnp.bfloat16),
            pltpu.VMEM((depth, nbasis), jnp.bfloat16),
            pltpu.SMEM(pattern.shape, jnp.int32),
            pltpu.VMEM((nbasis, nbasis), jnp.float32),
            pltpu.VMEM((nbasis, nbasis), jnp.float32),
            pltpu.VMEM((nbasis, depth), jnp.bfloat16),
            pltpu.SemaphoreType.DMA((3,)),
        ],
        compiler_params=params,
    )(*(pltpu.with_memory_space_constraint(a, pltpu.HBM) for a in inputs))
    side = jax.ShapeDtypeStruct((rows, nbasis), jnp.float32)
    sides = pl.pallas_call(
        side_kernel,
        out_shape=(side, side),
        in_specs=[vmem] * 2,
        out_specs=(vmem, vmem),
        cost_estimate=pl.CostEstimate(flops=100000, bytes_accessed=600000, transcendentals=0),
        compiler_params=params,
    )(parts[2:4], swap(parts[4:6]))
    first = swap(parts[6:8], FIRST, FIRST)
    near = [swap(sides[move[1]], move, move) for move in PLANE]
    own = parts[0:2] + first
    plane = [swap(own[1]), *near]
    line, far = pl.pallas_call(
        split_kernel,
        out_shape=(
            jax.ShapeDtypeStruct((3, rows, 128), jnp.float32),
            jax.ShapeDtypeStruct((rows // 2, nbasis), jnp.float32),
        ),
        in_specs=[vmem] * 4,
        out_specs=(vmem, vmem),
        compiler_params=params,
    )(own[0], *plane)
    far = swap(far, *FAR)
    near = swap(line[1], NEAR, NEAR)
    other = pl.pallas_call(
        pick_kernel,
        out_shape=jax.ShapeDtypeStruct((rows, 128), jnp.float32),
        in_specs=[vmem],
        out_specs=vmem,
        cost_estimate=pl.CostEstimate(flops=100_000, bytes_accessed=600_000, transcendentals=0),
        compiler_params=params,
    )(far)
    home = pl.pallas_call(
        home_kernel,
        out_shape=jax.ShapeDtypeStruct((rows, 128), jnp.float32),
        in_specs=[vmem] * 2,
        out_specs=vmem,
        cost_estimate=pl.CostEstimate(flops=100_000, bytes_accessed=600_000, transcendentals=0),
        compiler_params=params,
    )(line[0], far)
    return pl.pallas_call(
        turn_kernel,
        out_shape=jax.ShapeDtypeStruct((rows, cols), jnp.float32),
        in_specs=[vmem] * 3,
        out_specs=vmem,
        compiler_params=params,
    )(home, near, swap(other))


def any_shards(factors, response, pattern):
    nocc_dev, aux_dev, nbasis = factors.shape
    ground_rows = factors.reshape(nocc_dev * aux_dev, nbasis)
    response_rows = response.reshape(nocc_dev * aux_dev, nbasis)
    blk = nbasis // pattern.shape[0]
    own_cols = nbasis // lax.axis_size("occ")
    cross = lax.dot_general(
        ground_rows, response_rows, (((0,), (0,)), ((), ())), preferred_element_type=jnp.float32
    )
    masked = jnp.repeat(jnp.repeat(pattern.astype(jnp.float32), blk, axis=0), blk, axis=1) * cross
    both = 0.5 * (masked + masked.T)
    own_rows = lax.psum_scatter(both, "aux", scatter_dimension=0, tiled=True)
    summed = lax.psum(own_rows, "occ")
    return lax.dynamic_slice_in_dim(summed, lax.axis_index("occ") * own_cols, own_cols, 1)


def solution(mesh):
    in_specs = (P("occ", "aux", None), P("occ", "aux", None), P())
    out_specs = P("aux", "occ")
    sizes = dict(mesh.shape)
    shards = fast_shards if sizes["aux"] == 8 and sizes["occ"] == 4 else any_shards
    return jax.shard_map(shards, mesh=mesh, in_specs=in_specs, out_specs=out_specs, check_vma=False)
```

```python
import jax
import jax.numpy as jnp
from jax import lax
from jax.experimental import pallas as pl
from jax.experimental.pallas import tpu as pltpu
from jax.sharding import PartitionSpec as P

BOTH = ("aux", "occ")
FLIPS = (((1, 0, 0, 1), (1, 1, 0, 1)), ((0, 0, 1, 0), (0, 0, 0, 1)))
FLIP_BITS = sum(FLIPS[x][y][z] << (x * 8 + y * 4 + z) for x in range(2) for y in range(2) for z in range(4))
PLANE = ((1, 0, 0), (1, 1, 0))
FIRST = (0, 1, 0)
NEAR = (0, 0, 1)
FAR = ((0, 0, 3), (0, 0, 2))


def pairs(moves):
    if not moves:
        return [(i, i ^ 1) for i in range(32)]
    found = []
    for i in range(32):
        x, y, z, core = i >> 1 & 1, i >> 2 & 1, i >> 3, i & 1
        kind = core ^ FLIPS[x][y][z]
        move = moves[kind]
        x, y, z = x ^ move[0], y ^ move[1], z ^ move[2]
        found.append((i, ((z * 2 + y) * 2 + x) * 2 + (kind ^ FLIPS[x][y][z])))
    return found


def swap(value, *moves):
    return lax.ppermute(value, BOTH, pairs(moves))


def place():
    aux, occ = lax.axis_index("aux"), lax.axis_index("occ")
    return occ // 2, aux % 2, aux // 2, occ % 2


def product_kernel(pattern_hbm, ground_hbm, response_hbm, out_ref, ground, response, pattern, product, whole, turned, sems):
    nbasis = ground.shape[1]
    nblocks = pattern.shape[0]
    blk = nbasis // nblocks
    rows, cols = nbasis // 8, nbasis // 4

    first = pltpu.make_async_copy(ground_hbm, ground, sems.at[0])
    second = pltpu.make_async_copy(response_hbm, response, sems.at[1])
    masks = pltpu.make_async_copy(pattern_hbm, pattern, sems.at[2])
    first.start()
    second.start()
    masks.start()
    x, y, z, core = place()
    kind = core ^ (FLIP_BITS >> (x * 8 + y * 4 + z)) & 1
    first.wait()
    turned[...] = ground[...].T
    second.wait()
    masks.wait()
    block = lax.dot_general(turned[0:128, :], response[...], (((1,), (0,)), ((), ())), preferred_element_type=jnp.float32)
    for j in range(3):
        product[0:128, 128 * j : 128 * j + 128] = 0.5 * pattern[0, j].astype(jnp.float32) * block[:, 128 * j : 128 * j + 128]
    block = lax.dot_general(turned[128:256, :], response[...], (((1,), (0,)), ((), ())), preferred_element_type=jnp.float32)
    for j in range(3):
        product[128:256, 128 * j : 128 * j + 128] = 0.5 * pattern[1, j].astype(jnp.float32) * block[:, 128 * j : 128 * j + 128]
    block = lax.dot_general(turned[256:384, :], response[...], (((1,), (0,)), ((), ())), preferred_element_type=jnp.float32)
    for j in range(3):
        product[256:384, 128 * j : 128 * j + 128] = 0.5 * pattern[2, j].astype(jnp.float32) * block[:, 128 * j : 128 * j + 128]
    for i in range(nblocks):
        for j in range(nblocks):
            at_i, at_j = slice(i * blk, (i + 1) * blk), slice(j * blk, (j + 1) * blk)
            whole[at_i, at_j] = product[at_i, at_j] + product[at_j, at_i].T

    lane = lax.broadcasted_iota(jnp.int32, (8, nbasis), 1)
    even = sum((lane >= rows * k).astype(jnp.int32) for k in range(1, 8)) & 1 == 0
    z_to = sum((lane >= cols * k).astype(jnp.int32) for k in range(1, 4))
    left, two, three = z_to & 1 == 0, z_to == z ^ 2, z_to == z ^ 3
    mine = jnp.full_like(lane, kind) == 0

    def cut(at):
        return whole[at : at + rows, :].reshape(rows // 8, 8, nbasis)

    for x_to in range(2):
        turn = x ^ x_to
        upper, lower = ([cut(cols * (2 * x_to + c) + at) for c in range(2)] for at in (0, rows))
        for y_to in range(2):
            if y_to == 0:
                tiles = [jnp.where(even, u, pltpu.roll(d, rows, 2)) for u, d in zip(upper, lower)]
            else:
                tiles = [jnp.where(even, pltpu.roll(u, nbasis - rows, 2), d) for u, d in zip(upper, lower)]
            flips = lax.shift_right_logical(jnp.full_like(z_to, FLIP_BITS), x_to * 8 + y_to * 4 + z_to) & 1 == 0
            zero, one = jnp.where(flips, tiles[0], tiles[1]), jnp.where(flips, tiles[1], tiles[0])
            moved = jnp.where(three, one, zero)
            moved = jnp.where(left, pltpu.roll(moved, nbasis - cols, 2), pltpu.roll(moved, cols, 2))
            zero, one = jnp.where(two, moved, zero), jnp.where(three, moved, one)
            step = y ^ y_to
            own, other = jnp.where(mine, zero, one), jnp.where(mine, one, zero)
            out_ref[turn * (2 + step) + (1 - turn) * 6 * step, :, :] = own.reshape(rows, nbasis)
            out_ref[turn * (4 + step) + (1 - turn) * (1 + 6 * step), :, :] = other.reshape(rows, nbasis)


def side_kernel(own_ref, came_ref, x_ref, y_ref):
    x_ref[...] = own_ref[0] + came_ref[0]
    y_ref[...] = own_ref[1] + came_ref[1]


def split_kernel(own_ref, a_ref, b_ref, c_ref, tile_ref, far_ref):
    rows, nbasis = own_ref.shape
    cols, half = nbasis // 4, rows // 2
    total = own_ref[...] + a_ref[...] + b_ref[...] + c_ref[...]
    x, y, z, core = place()
    for z_to in range(4):
        tile_ref[jnp.minimum(z ^ z_to, 2), :, :cols] = total[:, cols * z_to : cols * (z_to + 1)]
    turned = pltpu.roll(total, nbasis // 2, 1)
    lane = lax.broadcasted_iota(jnp.int32, (half, nbasis), 1)
    low = lane < nbasis // 2
    high_far = jnp.full_like(lane, z // 2) == 0
    far_ref[...] = jnp.where(
        high_far, jnp.where(low, turned[:half], total[half:]), jnp.where(low, total[:half], turned[half:])
    )


def part_of(far_ref, parity):
    half, nbasis = far_ref.shape
    cols = nbasis // 4
    x, y, z, core = place()
    odd = jnp.full((half, cols), (z ^ parity) & 1) == 1
    first, second, third, fourth = (far_ref[:, cols * k : cols * (k + 1)] for k in range(4))
    return jnp.where(odd, second, first), jnp.where(odd, fourth, third)


def pick_kernel(far_ref, out_ref):
    half, cols = far_ref.shape[0], far_ref.shape[1] // 4
    out_ref[:half, :cols], out_ref[half:, :cols] = part_of(far_ref, 1)


def home_kernel(home_ref, far_ref, out_ref):
    half, cols = far_ref.shape[0], far_ref.shape[1] // 4
    top, bottom = part_of(far_ref, 0)
    out_ref[:half, :cols] = home_ref[:half, :cols] + top
    out_ref[half:, :cols] = home_ref[half:, :cols] + bottom


def turn_kernel(home_ref, near_ref, other_ref, out_ref):
    rows, cols = out_ref.shape
    total = home_ref[...] + near_ref[...] + other_ref[...]
    turned = total[:, :cols].T
    out_ref[...] = jnp.concatenate([turned[:rows], turned[rows:]], axis=1)


def fast_shards(factors, response, pattern):
    nocc_dev, aux_dev, nbasis = factors.shape
    depth = nocc_dev * aux_dev
    rows, cols = nbasis // 8, nbasis // 4
    vmem = pl.BlockSpec(memory_space=pltpu.VMEM)
    params = pltpu.CompilerParams(vmem_limit_bytes=32 * 1024 * 1024)
    inputs = (pattern, factors.reshape(depth, nbasis), response.reshape(depth, nbasis))
    parts = pl.pallas_call(
        product_kernel,
        out_shape=jax.ShapeDtypeStruct((8, rows, nbasis), jnp.float32),
        in_specs=[pl.BlockSpec(memory_space=pl.ANY)] * 3,
        out_specs=vmem,
        scratch_shapes=[
            pltpu.VMEM((depth, nbasis), jnp.bfloat16),
            pltpu.VMEM((depth, nbasis), jnp.bfloat16),
            pltpu.SMEM(pattern.shape, jnp.int32),
            pltpu.VMEM((nbasis, nbasis), jnp.float32),
            pltpu.VMEM((nbasis, nbasis), jnp.float32),
            pltpu.VMEM((nbasis, depth), jnp.bfloat16),
            pltpu.SemaphoreType.DMA((3,)),
        ],
        compiler_params=params,
    )(*(pltpu.with_memory_space_constraint(a, pltpu.HBM) for a in inputs))
    side = jax.ShapeDtypeStruct((rows, nbasis), jnp.float32)
    sides = pl.pallas_call(
        side_kernel,
        out_shape=(side, side),
        in_specs=[vmem] * 2,
        out_specs=(vmem, vmem),
        cost_estimate=pl.CostEstimate(flops=100000, bytes_accessed=600000, transcendentals=0),
        compiler_params=params,
    )(parts[2:4], swap(parts[4:6]))
    first = swap(parts[6:8], FIRST, FIRST)
    near = [swap(sides[move[1]], move, move) for move in PLANE]
    own = parts[0:2] + first
    plane = [swap(own[1]), *near]
    line, far = pl.pallas_call(
        split_kernel,
        out_shape=(
            jax.ShapeDtypeStruct((3, rows, 128), jnp.float32),
            jax.ShapeDtypeStruct((rows // 2, nbasis), jnp.float32),
        ),
        in_specs=[vmem] * 4,
        out_specs=(vmem, vmem),
        compiler_params=params,
    )(own[0], *plane)
    far = swap(far, *FAR)
    near = swap(line[1], NEAR, NEAR)
    other = pl.pallas_call(
        pick_kernel,
        out_shape=jax.ShapeDtypeStruct((rows, 128), jnp.float32),
        in_specs=[vmem],
        out_specs=vmem,
        cost_estimate=pl.CostEstimate(flops=100_000, bytes_accessed=600_000, transcendentals=0),
        compiler_params=params,
    )(far)
    home = pl.pallas_call(
        home_kernel,
        out_shape=jax.ShapeDtypeStruct((rows, 128), jnp.float32),
        in_specs=[vmem] * 2,
        out_specs=vmem,
        cost_estimate=pl.CostEstimate(flops=100_000, bytes_accessed=600_000, transcendentals=0),
        compiler_params=params,
    )(line[0], far)
    return pl.pallas_call(
        turn_kernel,
        out_shape=jax.ShapeDtypeStruct((rows, cols), jnp.float32),
        in_specs=[vmem] * 3,
        out_specs=vmem,
        compiler_params=params,
    )(home, near, swap(other))


def any_shards(factors, response, pattern):
    nocc_dev, aux_dev, nbasis = factors.shape
    ground_rows = factors.reshape(nocc_dev * aux_dev, nbasis)
    response_rows = response.reshape(nocc_dev * aux_dev, nbasis)
    blk = nbasis // pattern.shape[0]
    own_cols = nbasis // lax.axis_size("occ")
    cross = lax.dot_general(
        ground_rows, response_rows, (((0,), (0,)), ((), ())), preferred_element_type=jnp.float32
    )
    masked = jnp.repeat(jnp.repeat(pattern.astype(jnp.float32), blk, axis=0), blk, axis=1) * cross
    both = 0.5 * (masked + masked.T)
    own_rows = lax.psum_scatter(both, "aux", scatter_dimension=0, tiled=True)
    summed = lax.psum(own_rows, "occ")
    return lax.dynamic_slice_in_dim(summed, lax.axis_index("occ") * own_cols, own_cols, 1)


def solution(mesh):
    in_specs = (P("occ", "aux", None), P("occ", "aux", None), P())
    out_specs = P("aux", "occ")
    sizes = dict(mesh.shape)
    shards = fast_shards if sizes["aux"] == 8 and sizes["occ"] == 4 else any_shards
    return jax.shard_map(shards, mesh=mesh, in_specs=in_specs, out_specs=out_specs, check_vma=False)
```

```python
import jax
import jax.numpy as jnp
from jax import lax
from jax.experimental import pallas as pl
from jax.experimental.pallas import tpu as pltpu
from jax.sharding import PartitionSpec as P

BOTH = ("aux", "occ")
FLIPS = (((1, 0, 0, 1), (1, 1, 0, 1)), ((0, 0, 1, 0), (0, 0, 0, 1)))
FLIP_BITS = sum(FLIPS[x][y][z] << (x * 8 + y * 4 + z) for x in range(2) for y in range(2) for z in range(4))
PLANE = ((1, 0, 0), (1, 1, 0))
FIRST = (0, 1, 0)
NEAR = (0, 0, 1)
FAR = ((0, 0, 3), (0, 0, 2))


def pairs(moves):
    if not moves:
        return [(i, i ^ 1) for i in range(32)]
    found = []
    for i in range(32):
        x, y, z, core = i >> 1 & 1, i >> 2 & 1, i >> 3, i & 1
        kind = core ^ FLIPS[x][y][z]
        move = moves[kind]
        x, y, z = x ^ move[0], y ^ move[1], z ^ move[2]
        found.append((i, ((z * 2 + y) * 2 + x) * 2 + (kind ^ FLIPS[x][y][z])))
    return found


def swap(value, *moves):
    return lax.ppermute(value, BOTH, pairs(moves))


def place():
    aux, occ = lax.axis_index("aux"), lax.axis_index("occ")
    return occ // 2, aux % 2, aux // 2, occ % 2


def product_kernel(pattern_hbm, ground_hbm, response_hbm, out_ref, ground, response, pattern, product, whole, turned, sems):
    nbasis = ground.shape[1]
    nblocks = pattern.shape[0]
    blk = nbasis // nblocks
    rows, cols = nbasis // 8, nbasis // 4

    first = pltpu.make_async_copy(ground_hbm, ground, sems.at[0])
    second = pltpu.make_async_copy(response_hbm, response, sems.at[1])
    masks = pltpu.make_async_copy(pattern_hbm, pattern, sems.at[2])
    first.start()
    second.start()
    masks.start()
    x, y, z, core = place()
    kind = core ^ (FLIP_BITS >> (x * 8 + y * 4 + z)) & 1
    first.wait()
    turned[...] = ground[...].T
    second.wait()
    masks.wait()
    block = lax.dot_general(turned[0:128, :], response[...], (((1,), (0,)), ((), ())), preferred_element_type=jnp.float32)
    for j in range(3):
        product[0:128, 128 * j : 128 * j + 128] = 0.5 * pattern[0, j].astype(jnp.float32) * block[:, 128 * j : 128 * j + 128]
    block = lax.dot_general(turned[128:256, :], response[...], (((1,), (0,)), ((), ())), preferred_element_type=jnp.float32)
    for j in range(3):
        product[128:256, 128 * j : 128 * j + 128] = 0.5 * pattern[1, j].astype(jnp.float32) * block[:, 128 * j : 128 * j + 128]
    block = lax.dot_general(turned[256:384, :], response[...], (((1,), (0,)), ((), ())), preferred_element_type=jnp.float32)
    for j in range(3):
        product[256:384, 128 * j : 128 * j + 128] = 0.5 * pattern[2, j].astype(jnp.float32) * block[:, 128 * j : 128 * j + 128]
    for i in range(nblocks):
        for j in range(nblocks):
            at_i, at_j = slice(i * blk, (i + 1) * blk), slice(j * blk, (j + 1) * blk)
            whole[at_i, at_j] = product[at_i, at_j] + product[at_j, at_i].T

    lane = lax.broadcasted_iota(jnp.int32, (8, nbasis), 1)
    even = sum((lane >= rows * k).astype(jnp.int32) for k in range(1, 8)) & 1 == 0
    z_to = sum((lane >= cols * k).astype(jnp.int32) for k in range(1, 4))
    left, two, three = z_to & 1 == 0, z_to == z ^ 2, z_to == z ^ 3
    mine = jnp.full_like(lane, kind) == 0

    def cut(at):
        return whole[at : at + rows, :].reshape(rows // 8, 8, nbasis)

    for x_to in range(2):
        turn = x ^ x_to
        upper, lower = ([cut(cols * (2 * x_to + c) + at) for c in range(2)] for at in (0, rows))
        for y_to in range(2):
            if y_to == 0:
                tiles = [jnp.where(even, u, pltpu.roll(d, rows, 2)) for u, d in zip(upper, lower)]
            else:
                tiles = [jnp.where(even, pltpu.roll(u, nbasis - rows, 2), d) for u, d in zip(upper, lower)]
            flips = lax.shift_right_logical(jnp.full_like(z_to, FLIP_BITS), x_to * 8 + y_to * 4 + z_to) & 1 == 0
            zero, one = jnp.where(flips, tiles[0], tiles[1]), jnp.where(flips, tiles[1], tiles[0])
            moved = jnp.where(three, one, zero)
            moved = jnp.where(left, pltpu.roll(moved, nbasis - cols, 2), pltpu.roll(moved, cols, 2))
            zero, one = jnp.where(two, moved, zero), jnp.where(three, moved, one)
            step = y ^ y_to
            own, other = jnp.where(mine, zero, one), jnp.where(mine, one, zero)
            out_ref[turn * (2 + step) + (1 - turn) * 6 * step, :, :] = own.reshape(rows, nbasis)
            out_ref[turn * (4 + step) + (1 - turn) * (1 + 6 * step), :, :] = other.reshape(rows, nbasis)


def side_kernel(own_ref, came_ref, x_ref, y_ref):
    x_ref[...] = own_ref[0] + came_ref[0]
    y_ref[...] = own_ref[1] + came_ref[1]


def split_kernel(own_ref, a_ref, b_ref, c_ref, tile_ref, far_ref):
    rows, nbasis = own_ref.shape
    cols, half = nbasis // 4, rows // 2
    total = own_ref[...] + a_ref[...] + b_ref[...] + c_ref[...]
    x, y, z, core = place()
    for z_to in range(4):
        tile_ref[jnp.minimum(z ^ z_to, 2), :, :cols] = total[:, cols * z_to : cols * (z_to + 1)]
    lane = lax.broadcasted_iota(jnp.int32, (half, nbasis), 1)
    high_far = jnp.full_like(lane, z // 2) == 0
    moved = pltpu.roll(jnp.where(high_far, total[:half], total[half:]), nbasis // 2, 1)
    kept = jnp.where(high_far, total[half:], total[:half])
    low = (lane < nbasis // 2).astype(jnp.int32)
    far_ref[...] = jnp.where(low == high_far.astype(jnp.int32), moved, kept)


def part_of(far_ref, parity):
    half, nbasis = far_ref.shape
    cols = nbasis // 4
    x, y, z, core = place()
    odd = jnp.full((half, cols), (z ^ parity) & 1) == 1
    first, second, third, fourth = (far_ref[:, cols * k : cols * (k + 1)] for k in range(4))
    return jnp.where(odd, second, first), jnp.where(odd, fourth, third)


def pick_kernel(far_ref, out_ref):
    half, cols = far_ref.shape[0], far_ref.shape[1] // 4
    out_ref[:half, :cols], out_ref[half:, :cols] = part_of(far_ref, 1)


def home_kernel(home_ref, far_ref, out_ref):
    half, cols = far_ref.shape[0], far_ref.shape[1] // 4
    top, bottom = part_of(far_ref, 0)
    out_ref[:half, :cols] = home_ref[:half, :cols] + top
    out_ref[half:, :cols] = home_ref[half:, :cols] + bottom


def turn_kernel(home_ref, near_ref, other_ref, out_ref):
    rows, cols = out_ref.shape
    total = home_ref[...] + near_ref[...] + other_ref[...]
    turned = total[:, :cols].T
    out_ref[...] = jnp.concatenate([turned[:rows], turned[rows:]], axis=1)


def fast_shards(factors, response, pattern):
    nocc_dev, aux_dev, nbasis = factors.shape
    depth = nocc_dev * aux_dev
    rows, cols = nbasis // 8, nbasis // 4
    vmem = pl.BlockSpec(memory_space=pltpu.VMEM)
    params = pltpu.CompilerParams(vmem_limit_bytes=32 * 1024 * 1024)
    inputs = (pattern, factors.reshape(depth, nbasis), response.reshape(depth, nbasis))
    parts = pl.pallas_call(
        product_kernel,
        out_shape=jax.ShapeDtypeStruct((8, rows, nbasis), jnp.float32),
        in_specs=[pl.BlockSpec(memory_space=pl.ANY)] * 3,
        out_specs=vmem,
        scratch_shapes=[
            pltpu.VMEM((depth, nbasis), jnp.bfloat16),
            pltpu.VMEM((depth, nbasis), jnp.bfloat16),
            pltpu.SMEM(pattern.shape, jnp.int32),
            pltpu.VMEM((nbasis, nbasis), jnp.float32),
            pltpu.VMEM((nbasis, nbasis), jnp.float32),
            pltpu.VMEM((nbasis, depth), jnp.bfloat16),
            pltpu.SemaphoreType.DMA((3,)),
        ],
        compiler_params=params,
    )(*(pltpu.with_memory_space_constraint(a, pltpu.HBM) for a in inputs))
    side = jax.ShapeDtypeStruct((rows, nbasis), jnp.float32)
    sides = pl.pallas_call(
        side_kernel,
        out_shape=(side, side),
        in_specs=[vmem] * 2,
        out_specs=(vmem, vmem),
        cost_estimate=pl.CostEstimate(flops=100000, bytes_accessed=600000, transcendentals=0),
        compiler_params=params,
    )(parts[2:4], swap(parts[4:6]))
    first = swap(parts[6:8], FIRST, FIRST)
    near = [swap(sides[move[1]], move, move) for move in PLANE]
    own = parts[0:2] + first
    plane = [swap(own[1]), *near]
    line, far = pl.pallas_call(
        split_kernel,
        out_shape=(
            jax.ShapeDtypeStruct((3, rows, 128), jnp.float32),
            jax.ShapeDtypeStruct((rows // 2, nbasis), jnp.float32),
        ),
        in_specs=[vmem] * 4,
        out_specs=(vmem, vmem),
        compiler_params=params,
    )(own[0], *plane)
    far = swap(far, *FAR)
    near = swap(line[1], NEAR, NEAR)
    other = pl.pallas_call(
        pick_kernel,
        out_shape=jax.ShapeDtypeStruct((rows, 128), jnp.float32),
        in_specs=[vmem],
        out_specs=vmem,
        cost_estimate=pl.CostEstimate(flops=100_000, bytes_accessed=600_000, transcendentals=0),
        compiler_params=params,
    )(far)
    home = pl.pallas_call(
        home_kernel,
        out_shape=jax.ShapeDtypeStruct((rows, 128), jnp.float32),
        in_specs=[vmem] * 2,
        out_specs=vmem,
        cost_estimate=pl.CostEstimate(flops=100_000, bytes_accessed=600_000, transcendentals=0),
        compiler_params=params,
    )(line[0], far)
    return pl.pallas_call(
        turn_kernel,
        out_shape=jax.ShapeDtypeStruct((rows, cols), jnp.float32),
        in_specs=[vmem] * 3,
        out_specs=vmem,
        compiler_params=params,
    )(home, near, swap(other))


def any_shards(factors, response, pattern):
    nocc_dev, aux_dev, nbasis = factors.shape
    ground_rows = factors.reshape(nocc_dev * aux_dev, nbasis)
    response_rows = response.reshape(nocc_dev * aux_dev, nbasis)
    blk = nbasis // pattern.shape[0]
    own_cols = nbasis // lax.axis_size("occ")
    cross = lax.dot_general(
        ground_rows, response_rows, (((0,), (0,)), ((), ())), preferred_element_type=jnp.float32
    )
    masked = jnp.repeat(jnp.repeat(pattern.astype(jnp.float32), blk, axis=0), blk, axis=1) * cross
    both = 0.5 * (masked + masked.T)
    own_rows = lax.psum_scatter(both, "aux", scatter_dimension=0, tiled=True)
    summed = lax.psum(own_rows, "occ")
    return lax.dynamic_slice_in_dim(summed, lax.axis_index("occ") * own_cols, own_cols, 1)


def solution(mesh):
    in_specs = (P("occ", "aux", None), P("occ", "aux", None), P())
    out_specs = P("aux", "occ")
    sizes = dict(mesh.shape)
    shards = fast_shards if sizes["aux"] == 8 and sizes["occ"] == 4 else any_shards
    return jax.shard_map(shards, mesh=mesh, in_specs=in_specs, out_specs=out_specs, check_vma=False)
```
